32 devices in a mesh: layer: 2 (over y), row: 4 (over z), col: 4 (over x, core).
Axes of the slice: x: 2, y: 2, z: 4, core: 2. Of those that a mesh axis runs over, the one named last changes fastest.
Arguments:
- factor: float32 [32, 4, 256, 2048], P('layer', 'row', None, 'col'), parts along dimension 0, may hold values from -1 to 4, as said below
- gradient: bfloat16 [32, 4, 256, 4096], P('layer', 'row', None, 'col'), parts along dimension 0, may hold values from -6 to 6
Outputs:
- solution: float32 [32, 4, 256, 4096], P('layer', 'row', None, 'col'), parts along dimension 0
The draws below stay inside these ranges and needn't reach their ends.
There are 2 independent parts, one for each index of `layer`. The reference program is written for one: setup_inputs(seed, part) draws one part's arguments, and reference() takes and returns one part's arrays. A program takes and returns all parts, laid end to end along the dimension named above; each array names one. Nothing has to cross between parts.
Inputs may be any that keep to these rules, and one draw needn't show every extreme that they name: The factor is lower triangular: the entry of whole row i and column j is zero for j > i, and the diagonal lies between 1 and 4.
All inputs are finite; a program needn't handle non-finite values.
Results may differ from the reference program's by a relative error of at most 0.0039.
Values may be sent and summed in bfloat16 or wider, within the bound.
A program may use at most 128 MiB of HBM per device.

```python
import jax
import jax.numpy as jnp
from jax import lax

ORDER = 16384
COLS = 4096
BLOCK = 256
STEPS = 8
CYCLES = 16
PANEL = 2048
N_ROW = 4


def draw_factor(key, part):
    key = jax.random.fold_in(key, 11)
    first_key, second_key = jax.random.split(key, 2)
    array_shape = (CYCLES, N_ROW, BLOCK, PANEL)
    row_shape = (CYCLES, N_ROW, BLOCK, 1)
    cycle_ids = jnp.arange(CYCLES).reshape(CYCLES, 1, 1, 1)
    device_ids = jnp.arange(N_ROW).reshape(1, N_ROW, 1, 1)
    inner_ids = jnp.arange(BLOCK).reshape(1, 1, BLOCK, 1)
    global_row = (cycle_ids * N_ROW + device_ids) * BLOCK + inner_ids
    column_ids = jnp.arange(PANEL).reshape(1, 1, 1, PANEL)
    noise_values = jnp.clip(jax.random.normal(first_key, array_shape, jnp.float32), -4.0, 4.0)
    diagonal = jax.random.uniform(second_key, row_shape, jnp.float32, 1.0, 2.0)
    same_block = column_ids // BLOCK == global_row // BLOCK
    entry_scale = jnp.where(same_block, 0.5 / BLOCK ** 0.5, 0.6 / PANEL ** 0.5)
    values = jnp.where(column_ids < global_row, noise_values * entry_scale, 0.0)
    values = jnp.where(column_ids == global_row - 1, 0.4 * diagonal, values)
    values = jnp.where(column_ids == global_row - BLOCK, 0.45 * diagonal, values)
    values = jnp.where(column_ids == global_row, diagonal, values)
    return values.astype(jnp.float32)


def shard_levels(stream_key, dims, cuts, smallest, largest):
    gain = 1.0
    for dim, parts in cuts:
        draws = jax.random.uniform(jax.random.fold_in(jax.random.fold_in(stream_key, 6), dim), (parts,), jnp.float32, smallest / len(cuts), largest / len(cuts))
        gain = gain * jnp.repeat(jnp.exp(draws), dims[dim] // parts).reshape((-1,) + (1,) * (len(dims) - 1 - dim))
    return gain


def bell_draw(own_key, shape, width, limit, cuts=(), held_as=jnp.bfloat16):
    array = width * jax.random.normal(own_key, shape, jnp.float32)
    if cuts:
        array = array * shard_levels(own_key, shape, cuts, -0.22, 0.18)
    return jnp.clip(array, -limit, limit).astype(held_as)


def setup_inputs(seed: int = 0, part: int = 0) -> dict:
    splits = jax.random.split(jax.random.key(seed), 3)
    part_splits = jax.random.split(jax.random.fold_in(splits[2], part), 3)
    return {
        "factor": draw_factor(jax.random.fold_in(jax.random.fold_in(splits[2], part), 71), part),
        "gradient": bell_draw(part_splits[1], (CYCLES, N_ROW, BLOCK, COLS), 1.0, 6.0, ((1, 4), (3, 4))),
    }


def solve_diagonal(diagonal, right_side):
    return lax.linalg.triangular_solve(diagonal, right_side, left_side=True, lower=True)

def reference(factor, gradient):
    lowered = lax.optimization_barrier(factor.reshape(ORDER, PANEL).astype(jnp.bfloat16)).astype(jnp.float32)
    right_side = gradient.reshape(ORDER, COLS).astype(jnp.float32)
    solved_rows = []
    rounded_rows = []
    for position in range(STEPS):
        row_start = position * BLOCK
        partial_side = right_side[row_start:row_start + BLOCK]
        if position > 0:
            earlier = jnp.concatenate(rounded_rows, axis=0)
            partial_side = partial_side - jnp.dot(lowered[row_start:row_start + BLOCK, :row_start], earlier, precision=lax.Precision.HIGHEST)
        diagonal = lowered[row_start:row_start + BLOCK, row_start:row_start + BLOCK]
        solved = solve_diagonal(diagonal, partial_side)
        solved_rows.append(solved)
        rounded_rows.append(lax.optimization_barrier(solved.astype(jnp.bfloat16)).astype(jnp.float32))
    every_rounded = jnp.concatenate(rounded_rows, axis=0)
    trailing = right_side[PANEL:] - jnp.dot(lowered[PANEL:], every_rounded, precision=lax.Precision.HIGHEST)
    whole = jnp.concatenate(solved_rows + [trailing], axis=0)
    return whole.reshape(CYCLES, N_ROW, BLOCK, COLS)
```

```python
import functools

import jax
import jax.numpy as jnp
from jax import lax
from jax.experimental import pallas as pl
from jax.experimental.pallas import tpu as pltpu
from jax.sharding import PartitionSpec as P

STEPS = 8
ROWS = 4
COLS = 4
SPLIT = 4
HALF = 128
GROUP = 2
MESH = pl.DeviceIdType.MESH

def broadcast(shard, axis, root):
    mine = lax.axis_index(axis) == root
    return lax.psum(jnp.where(mine, shard, jnp.zeros_like(shard)), axis)


def general(factor, gradient):
    row_count = lax.axis_size("row")
    my_row = lax.axis_index("row")
    cycles, _, block_size, width_local = factor.shape
    blocks_per = width_local // block_size
    lowered = factor.reshape(cycles * block_size, width_local).astype(jnp.bfloat16)
    current = gradient.reshape(cycles * block_size, gradient.shape[3]).astype(jnp.float32)
    row_blocks = jnp.arange(cycles * block_size, dtype=jnp.int32) // block_size * row_count + my_row

    def fetch_tile(position):
        own_part = lax.dynamic_slice_in_dim(
            lowered, position % blocks_per * block_size, block_size, 1
        )
        return broadcast(own_part, "col", position // blocks_per)

    def own_rows(array, position):
        return lax.dynamic_slice_in_dim(array, position // row_count * block_size, block_size, 0)

    def solve_at(position, column_tile, right_side):
        diagonal = own_rows(column_tile, position).astype(jnp.float32)
        is_owner = position % row_count == my_row
        diagonal = jnp.where(is_owner, diagonal, jnp.eye(block_size, dtype=jnp.float32))
        return lax.linalg.triangular_solve(diagonal, right_side, left_side=True, lower=True)

    def share(solved, position):
        return broadcast(solved.astype(jnp.bfloat16), "row", position % row_count)

    def apply_block(current, position, column_tile, solved, sent_block):
        stored = lax.dynamic_update_slice_in_dim(
            current, solved, position // row_count * block_size, 0
        )
        is_owner = position % row_count == my_row
        current = jnp.where(is_owner, stored, current)
        product = jnp.dot(column_tile, sent_block, preferred_element_type=jnp.float32)
        pending = (row_blocks > position)[:, None]
        return current - jnp.where(pending, product, 0.0)

    def advance(position, current):
        column_tile = fetch_tile(position)
        solved = solve_at(position, column_tile, own_rows(current, position))
        sent_block = share(solved, position)
        return apply_block(current, position, column_tile, solved, sent_block)

    current = lax.fori_loop(0, STEPS, advance, current)
    return current.reshape(gradient.shape)


def exact_dot(a, b):
    return jnp.dot(a, b, precision=lax.Precision.HIGHEST, preferred_element_type=jnp.float32)


def invert_lower(lower):
    size = lower.shape[0]
    row = lax.broadcasted_iota(jnp.int32, (size, size), 0)
    col = lax.broadcasted_iota(jnp.int32, (size, size), 1)
    diagonal = jnp.where(row == col, lower, 0.0)
    scale_col = 1.0 / jnp.sum(diagonal, axis=0, keepdims=True)
    scale_row = 1.0 / jnp.sum(diagonal, axis=1, keepdims=True)
    pair = (row == col + 1) & (row % 2 == 1)
    inverse = jnp.where(row == col, scale_row, 0.0) - jnp.where(
        pair, scale_row * lower * scale_col, 0.0
    )
    width = 2
    while width < size:
        below = (
            (row // (2 * width) == col // (2 * width))
            & ((row // width) % 2 == 1)
            & ((col // width) % 2 == 0)
        )
        step = exact_dot(jnp.where(below, lower, 0.0), inverse)
        inverse = inverse - exact_dot(inverse, step)
        width *= 2
    return inverse


def solve_kernel(
    panel, grad, gathered, every_solved, own_solved,
    top, solved, inverse,
    x_send, x_recv, s_send, s_recv, f_send, f_recv,
    up_send, down_send, z_recv, local_sem,
):
    col = lax.axis_index("col")
    row = lax.axis_index("row")
    block = top.shape[2]
    chunk = solved.shape[2]
    heads = top.shape[1]
    groups = gathered.shape[1] // GROUP
    partner = (col + 2) % COLS
    sibling = col + 1 - 2 * (col % 2)

    barrier = pltpu.get_barrier_semaphore()
    for other in (partner, sibling):
        pl.semaphore_signal(barrier, inc=1, device_id={"col": other}, device_id_type=MESH)

    @pl.when(row > 0)
    def _():
        pl.semaphore_signal(barrier, inc=1, device_id={"row": row - 1}, device_id_type=MESH)

    @pl.when(row < ROWS - 1)
    def _():
        pl.semaphore_signal(barrier, inc=1, device_id={"row": row + 1}, device_id_type=MESH)

    inner = (row > 0) & (row < ROWS - 1)

    @pl.when(inner)
    def _():
        pl.semaphore_wait(barrier, 4)

    @pl.when(jnp.logical_not(inner))
    def _():
        pl.semaphore_wait(barrier, 3)

    def place(slab, item):
        if isinstance(item, int) and item < heads:
            return top.at[slab, item]
        return gathered.at[slab, pl.ds((item - heads) * GROUP, GROUP)]

    def source(item):
        if isinstance(item, int) and item < heads:
            return panel.at[item]
        return panel.at[pl.ds(heads + (item - heads) * GROUP, GROUP)]

    def to_partner(item):
        return pltpu.make_async_remote_copy(
            src_ref=source(item), dst_ref=place(col, item),
            send_sem=x_send.at[item], recv_sem=x_recv.at[item],
            device_id={"col": partner}, device_id_type=MESH,
        )

    def to_sibling(item):
        return pltpu.make_async_remote_copy(
            src_ref=source(item), dst_ref=place(col, item),
            send_sem=s_send.at[item], recv_sem=s_recv.at[item],
            device_id={"col": sibling}, device_id_type=MESH,
        )

    def forward(item):
        return pltpu.make_async_remote_copy(
            src_ref=place(partner, item), dst_ref=place(partner, item),
            send_sem=f_send.at[item], recv_sem=f_recv.at[item],
            device_id={"col": sibling}, device_id_type=MESH,
        )

    def pass_on(item):
        to_partner(item).wait_recv()
        forward(item).start()

    def keep_head(item):
        return pltpu.make_async_copy(panel.at[item], top.at[col, item], local_sem.at[item])

    keep_rest = pltpu.make_async_copy(
        panel.at[pl.ds(heads, groups * GROUP)], gathered.at[col], local_sem.at[heads]
    )

    for item in range(heads):
        to_partner(item).start()
        to_sibling(item).start()
        keep_head(item).start()

    def receive_head(item):
        keep_head(item).wait()
        pass_on(item)
        to_sibling(item).wait_recv()
        forward(item).wait_recv()

    def invert(index):
        slab = row // 2 + 2 * index
        for half in range(2):
            start = pl.multiple_of((row % 2) * block + half * HALF, HALF)
            diagonal = top[slab, index, half * HALF:(half + 1) * HALF, pl.ds(start, HALF)]
            inverse[index, half] = invert_lower(diagonal.astype(jnp.float32))

    receive_head(0)

    @pl.loop(heads, heads + groups)
    def _(item):
        to_partner(item).start()

    invert(0)
    receive_head(1)

    @pl.when(row > 0)
    def _():
        invert(1)

    @pl.loop(heads, heads + groups)
    def _(item):
        to_sibling(item).start()

    keep_rest.start()

    def send_row(position, part, step, sems):
        piece = solved.at[part, pl.ds(position * block, block)]
        return pltpu.make_async_remote_copy(
            src_ref=piece, dst_ref=piece,
            send_sem=sems.at[position * SPLIT + part],
            recv_sem=z_recv.at[position * SPLIT + part],
            device_id={"row": row + step}, device_id_type=MESH,
        )

    def solve(position, part):
        index = position // ROWS
        columns = pl.ds(pl.multiple_of(part * chunk, chunk), chunk)
        right = grad[index, :, columns].astype(jnp.float32)
        width = top.shape[3]
        done = 0
        while done < position * block:
            take = min(width, position * block - done)
            right = right - jnp.dot(
                top[done // width, index, :, 0:take],
                solved[part, done:done + take, :],
                preferred_element_type=jnp.float32,
            )
            done += take
        first = exact_dot(inverse[index, 0], right[:HALF])
        slab, start = position * block // width, position * block % width
        below = top[slab, index, HALF:, start:start + HALF].astype(jnp.float32)
        second = exact_dot(inverse[index, 1], right[HALF:] - exact_dot(below, first))
        own_solved[index, :HALF, columns] = first
        own_solved[index, HALF:, columns] = second
        base = position * block
        solved[part, base:base + HALF, :] = first.astype(jnp.bfloat16)
        solved[part, base + HALF:base + block, :] = second.astype(jnp.bfloat16)

    def for_sends(position, part, act):
        owner = position % ROWS

        @pl.when((row >= owner) & (row < ROWS - 1))
        def _():
            act(send_row(position, part, 1, up_send))

        @pl.when((row <= owner) & (row > 0))
        def _():
            act(send_row(position, part, -1, down_send))

    @pl.loop(0, STEPS + SPLIT - 1)
    def _(wave):
        for position in range(STEPS):
            part = wave - position

            @pl.when((part >= 0) & (part < SPLIT))
            def _():
                @pl.when(row == position % ROWS)
                def _():
                    solve(position, part)

                @pl.when(row != position % ROWS)
                def _():
                    send_row(position, part, 0, up_send).wait_recv()

                for_sends(position, part, lambda copy: copy.start())

        @pl.when((wave == ROWS - 1) & (row == 0))
        def _():
            invert(1)

        @pl.when((wave % 2 == 1) & (wave // 2 < groups))
        def _():
            pass_on(heads + wave // 2)

    passed = min(groups, (STEPS + SPLIT - 1) // 2)

    write_solved = pltpu.make_async_copy(solved, every_solved, local_sem.at[heads + 1])
    write_solved.start()

    @pl.loop(heads + passed, heads + groups)
    def _(item):
        pass_on(item)

    for item in range(heads):
        to_partner(item).wait_send()
        to_sibling(item).wait_send()
        forward(item).wait_send()

    @pl.loop(heads, heads + groups)
    def _(item):
        to_partner(item).wait_send()
        to_sibling(item).wait()
        forward(item).wait()

    for position in range(STEPS):
        @pl.loop(0, SPLIT)
        def _(part):
            for_sends(position, part, lambda copy: copy.wait_send())

    keep_rest.wait()
    write_solved.wait()


def trailing_kernel(heads, gathered, every_solved, own_solved, grad, out):
    cycle = pl.program_id(0)

    @pl.when(cycle < heads)
    def _():
        out[0] = own_solved[0]

    @pl.when(cycle >= heads)
    def _():
        chunk = every_solved.shape[2]
        width = gathered.shape[3]
        for part in range(every_solved.shape[0]):
            columns = slice(part * chunk, (part + 1) * chunk)
            total = grad[0, :, columns].astype(jnp.float32)
            for slab in range(gathered.shape[0]):
                total = total - jnp.dot(
                    gathered[slab, 0],
                    every_solved[part, slab * width:(slab + 1) * width, :],
                    preferred_element_type=jnp.float32,
                )
            out[0, :, columns] = total


def fused(factor, gradient):
    cycles, _, block, width = factor.shape
    columns = gradient.shape[3]
    heads = STEPS // ROWS
    chunk = columns // SPLIT
    items = heads + (cycles - heads) // GROUP
    panel = factor.reshape(cycles, block, width).astype(jnp.bfloat16)
    grad = gradient.reshape(cycles, block, columns)
    dma = pltpu.SemaphoreType.DMA
    any_spec = pl.BlockSpec(memory_space=pl.ANY)
    vmem_spec = pl.BlockSpec(memory_space=pltpu.VMEM)
    gathered, every_solved, own_solved = pl.pallas_call(
        solve_kernel,
        out_shape=(
            jax.ShapeDtypeStruct((COLS, cycles - heads, block, width), jnp.bfloat16),
            jax.ShapeDtypeStruct((SPLIT, STEPS * block, chunk), jnp.bfloat16),
            jax.ShapeDtypeStruct((heads, block, columns), jnp.float32),
        ),
        in_specs=[any_spec, vmem_spec],
        out_specs=(any_spec, any_spec, vmem_spec),
        scratch_shapes=[
            pltpu.VMEM((COLS, heads, block, width), jnp.bfloat16),
            pltpu.VMEM((SPLIT, STEPS * block, chunk), jnp.bfloat16),
            pltpu.VMEM((heads, 2, HALF, HALF), jnp.float32),
        ]
        + [dma((items,))] * 6
        + [dma((STEPS * SPLIT,))] * 3
        + [dma((heads + 2,))],
        compiler_params=pltpu.CompilerParams(
            collective_id=0, has_side_effects=True, vmem_limit_bytes=56 * 1024 * 1024
        ),
    )(panel, grad[:heads])
    out = pl.pallas_call(
        functools.partial(trailing_kernel, heads),
        grid=(cycles,),
        out_shape=jax.ShapeDtypeStruct((cycles, block, columns), jnp.float32),
        in_specs=[
            pl.BlockSpec((COLS, 1, block, width), lambda i: (0, jnp.maximum(i - heads, 0), 0, 0)),
            pl.BlockSpec((SPLIT, STEPS * block, chunk), lambda i: (0, 0, 0)),
            pl.BlockSpec((1, block, columns), lambda i: (jnp.minimum(i, heads - 1), 0, 0)),
            pl.BlockSpec((1, block, columns), lambda i: (i, 0, 0)),
        ],
        out_specs=pl.BlockSpec((1, block, columns), lambda i: (i, 0, 0)),
        compiler_params=pltpu.CompilerParams(
            dimension_semantics=("arbitrary",), vmem_limit_bytes=56 * 1024 * 1024
        ),
    )(gathered, every_solved, own_solved, grad)
    return out.reshape(gradient.shape)


def local(factor, gradient):
    cycles, _, block, width = factor.shape
    fits = (
        lax.axis_size("row") == ROWS
        and lax.axis_size("col") == COLS
        and width == 2 * block
        and block == 2 * HALF
        and COLS * width == STEPS * block
        and (cycles - STEPS // ROWS) % GROUP == 0
    )
    return fused(factor, gradient) if fits else general(factor, gradient)


def solution(mesh):
    return jax.shard_map(
        local,
        mesh=mesh,
        in_specs=(P("layer", "row", None, "col"), P("layer", "row", None, "col")),
        out_specs=P("layer", "row", None, "col"),
        check_vma=False,
    )
```

```python
import functools

import jax
import jax.numpy as jnp
from jax import lax
from jax.experimental import pallas as pl
from jax.experimental.pallas import tpu as pltpu
from jax.sharding import PartitionSpec as P

STEPS = 8
ROWS = 4
COLS = 4
SPLIT = 4
HALF = 128
GROUP = 2
MESH = pl.DeviceIdType.MESH

def broadcast(shard, axis, root):
    mine = lax.axis_index(axis) == root
    return lax.psum(jnp.where(mine, shard, jnp.zeros_like(shard)), axis)


def general(factor, gradient):
    row_count = lax.axis_size("row")
    my_row = lax.axis_index("row")
    cycles, _, block_size, width_local = factor.shape
    blocks_per = width_local // block_size
    lowered = factor.reshape(cycles * block_size, width_local).astype(jnp.bfloat16)
    current = gradient.reshape(cycles * block_size, gradient.shape[3]).astype(jnp.float32)
    row_blocks = jnp.arange(cycles * block_size, dtype=jnp.int32) // block_size * row_count + my_row

    def fetch_tile(position):
        own_part = lax.dynamic_slice_in_dim(
            lowered, position % blocks_per * block_size, block_size, 1
        )
        return broadcast(own_part, "col", position // blocks_per)

    def own_rows(array, position):
        return lax.dynamic_slice_in_dim(array, position // row_count * block_size, block_size, 0)

    def solve_at(position, column_tile, right_side):
        diagonal = own_rows(column_tile, position).astype(jnp.float32)
        is_owner = position % row_count == my_row
        diagonal = jnp.where(is_owner, diagonal, jnp.eye(block_size, dtype=jnp.float32))
        return lax.linalg.triangular_solve(diagonal, right_side, left_side=True, lower=True)

    def share(solved, position):
        return broadcast(solved.astype(jnp.bfloat16), "row", position % row_count)

    def apply_block(current, position, column_tile, solved, sent_block):
        stored = lax.dynamic_update_slice_in_dim(
            current, solved, position // row_count * block_size, 0
        )
        is_owner = position % row_count == my_row
        current = jnp.where(is_owner, stored, current)
        product = jnp.dot(column_tile, sent_block, preferred_element_type=jnp.float32)
        pending = (row_blocks > position)[:, None]
        return current - jnp.where(pending, product, 0.0)

    def advance(position, current):
        column_tile = fetch_tile(position)
        solved = solve_at(position, column_tile, own_rows(current, position))
        sent_block = share(solved, position)
        return apply_block(current, position, column_tile, solved, sent_block)

    current = lax.fori_loop(0, STEPS, advance, current)
    return current.reshape(gradient.shape)


def exact_dot(a, b):
    return jnp.dot(a, b, precision=lax.Precision.HIGHEST, preferred_element_type=jnp.float32)


def invert_lower(lower):
    size = lower.shape[0]
    row = lax.broadcasted_iota(jnp.int32, (size, size), 0)
    col = lax.broadcasted_iota(jnp.int32, (size, size), 1)
    diagonal = jnp.where(row == col, lower, 0.0)
    scale_col = 1.0 / jnp.sum(diagonal, axis=0, keepdims=True)
    scale_row = 1.0 / jnp.sum(diagonal, axis=1, keepdims=True)
    pair = (row == col + 1) & (row % 2 == 1)
    inverse = jnp.where(row == col, scale_row, 0.0) - jnp.where(
        pair, scale_row * lower * scale_col, 0.0
    )
    width = 2
    while width < size:
        below = (
            (row // (2 * width) == col // (2 * width))
            & ((row // width) % 2 == 1)
            & ((col // width) % 2 == 0)
        )
        step = exact_dot(jnp.where(below, lower, 0.0), inverse)
        inverse = inverse - exact_dot(inverse, step)
        width *= 2
    return inverse


def solve_kernel(
    panel, grad, gathered, every_solved, own_solved,
    top, solved, inverse,
    x_send, x_recv, s_send, s_recv, f_send, f_recv,
    up_send, down_send, z_recv, local_sem,
):
    col = lax.axis_index("col")
    row = lax.axis_index("row")
    block = top.shape[2]
    chunk = solved.shape[2]
    heads = top.shape[1]
    groups = gathered.shape[1] // GROUP
    partner = (col + 2) % COLS
    sibling = col + 1 - 2 * (col % 2)

    barrier = pltpu.get_barrier_semaphore()
    for other in (partner, sibling):
        pl.semaphore_signal(barrier, inc=1, device_id={"col": other}, device_id_type=MESH)

    @pl.when(row > 0)
    def _():
        pl.semaphore_signal(barrier, inc=1, device_id={"row": row - 1}, device_id_type=MESH)

    @pl.when(row < ROWS - 1)
    def _():
        pl.semaphore_signal(barrier, inc=1, device_id={"row": row + 1}, device_id_type=MESH)

    inner = (row > 0) & (row < ROWS - 1)

    @pl.when(inner)
    def _():
        pl.semaphore_wait(barrier, 4)

    @pl.when(jnp.logical_not(inner))
    def _():
        pl.semaphore_wait(barrier, 3)

    def place(slab, slot, item):
        if isinstance(item, int) and item < heads:
            return top.at[slab, item]
        return gathered.at[slot, pl.ds((item - heads) * GROUP, GROUP)]

    def source(item):
        if isinstance(item, int) and item < heads:
            return panel.at[item]
        return panel.at[pl.ds(heads + (item - heads) * GROUP, GROUP)]

    def to_partner(item):
        return pltpu.make_async_remote_copy(
            src_ref=source(item), dst_ref=place(col, 0, item),
            send_sem=x_send.at[item], recv_sem=x_recv.at[item],
            device_id={"col": partner}, device_id_type=MESH,
        )

    def to_sibling(item):
        return pltpu.make_async_remote_copy(
            src_ref=source(item), dst_ref=place(col, 1, item),
            send_sem=s_send.at[item], recv_sem=s_recv.at[item],
            device_id={"col": sibling}, device_id_type=MESH,
        )

    def forward(item):
        return pltpu.make_async_remote_copy(
            src_ref=place(partner, 0, item), dst_ref=place(partner, 2, item),
            send_sem=f_send.at[item], recv_sem=f_recv.at[item],
            device_id={"col": sibling}, device_id_type=MESH,
        )

    def pass_on(item):
        to_partner(item).wait_recv()
        forward(item).start()

    def keep_head(item):
        return pltpu.make_async_copy(panel.at[item], top.at[col, item], local_sem.at[item])

    for item in range(heads):
        to_partner(item).start()
        to_sibling(item).start()
        keep_head(item).start()

    def receive_head(item):
        keep_head(item).wait()
        pass_on(item)
        to_sibling(item).wait_recv()
        forward(item).wait_recv()

    def invert(index):
        slab = row // 2 + 2 * index
        for half in range(2):
            start = pl.multiple_of((row % 2) * block + half * HALF, HALF)
            diagonal = top[slab, index, half * HALF:(half + 1) * HALF, pl.ds(start, HALF)]
            inverse[index, half] = invert_lower(diagonal.astype(jnp.float32))

    receive_head(0)

    @pl.loop(heads, heads + groups)
    def _(item):
        to_partner(item).start()

    invert(0)
    receive_head(1)

    @pl.when(row > 0)
    def _():
        invert(1)

    @pl.loop(heads, heads + groups)
    def _(item):
        to_sibling(item).start()

    def send_row(position, part, step, sems):
        piece = solved.at[part, pl.ds(position * block, block)]
        return pltpu.make_async_remote_copy(
            src_ref=piece, dst_ref=piece,
            send_sem=sems.at[position * SPLIT + part],
            recv_sem=z_recv.at[position * SPLIT + part],
            device_id={"row": row + step}, device_id_type=MESH,
        )

    def solve(position, part):
        index = position // ROWS
        columns = pl.ds(pl.multiple_of(part * chunk, chunk), chunk)
        right = grad[index, :, columns].astype(jnp.float32)
        width = top.shape[3]
        done = 0
        while done < position * block:
            take = min(width, position * block - done)
            right = right - jnp.dot(
                top[done // width, index, :, 0:take],
                solved[part, done:done + take, :],
                preferred_element_type=jnp.float32,
            )
            done += take
        first = exact_dot(inverse[index, 0], right[:HALF])
        slab, start = position * block // width, position * block % width
        below = top[slab, index, HALF:, start:start + HALF].astype(jnp.float32)
        second = exact_dot(inverse[index, 1], right[HALF:] - exact_dot(below, first))
        own_solved[index, :HALF, columns] = first
        own_solved[index, HALF:, columns] = second
        base = position * block
        solved[part, base:base + HALF, :] = first.astype(jnp.bfloat16)
        solved[part, base + HALF:base + block, :] = second.astype(jnp.bfloat16)

    def for_sends(position, part, act):
        owner = position % ROWS

        @pl.when((row >= owner) & (row < ROWS - 1))
        def _():
            act(send_row(position, part, 1, up_send))

        @pl.when((row <= owner) & (row > 0))
        def _():
            act(send_row(position, part, -1, down_send))

    starts = [0]
    for position in range(1, STEPS):
        hops = abs(position % ROWS - (position - 1) % ROWS)
        starts.append(starts[-1] + 1 + hops)
    ticks = starts[-1] + SPLIT + ROWS

    @pl.loop(0, ticks)
    def _(tick):
        for position in range(STEPS):
            hops = jnp.abs(row - position % ROWS)
            part = tick - starts[position] - jnp.where(hops == 0, 0, 1 + hops)

            @pl.when((part >= 0) & (part < SPLIT))
            def _():
                @pl.when(row == position % ROWS)
                def _():
                    solve(position, part)

                @pl.when(row != position % ROWS)
                def _():
                    send_row(position, part, 0, up_send).wait_recv()

                for_sends(position, part, lambda copy: copy.start())

        @pl.when((tick == SPLIT - 1) & (row == 0))
        def _():
            invert(1)

        @pl.when((tick % 3 == 2) & (tick // 3 < groups))
        def _():
            pass_on(heads + tick // 3)

    passed = min(groups, ticks // 3)

    write_solved = pltpu.make_async_copy(solved, every_solved, local_sem.at[heads])
    write_solved.start()

    @pl.loop(heads + passed, heads + groups)
    def _(item):
        pass_on(item)

    for item in range(heads):
        to_partner(item).wait_send()
        to_sibling(item).wait_send()
        forward(item).wait_send()

    @pl.loop(heads, heads + groups)
    def _(item):
        to_partner(item).wait_send()
        to_sibling(item).wait()
        forward(item).wait()

    for position in range(STEPS):
        @pl.loop(0, SPLIT)
        def _(part):
            for_sends(position, part, lambda copy: copy.wait_send())

    write_solved.wait()


def trailing_kernel(heads, panel, gathered, every_solved, own_solved, grad, out):
    col = lax.axis_index("col")
    cycle = pl.program_id(0)

    @pl.when(cycle < heads)
    def _():
        out[0] = own_solved[0]

    @pl.when(cycle >= heads)
    def _():
        chunk = every_solved.shape[2]
        width = gathered.shape[3]
        sibling = col + 1 - 2 * (col % 2)
        slabs = (col, (col + 2) % COLS, sibling, (sibling + 2) % COLS)
        lefts = (panel[0], gathered[0, 0], gathered[1, 0], gathered[2, 0])
        for part in range(every_solved.shape[0]):
            columns = slice(part * chunk, (part + 1) * chunk)
            total = grad[0, :, columns].astype(jnp.float32)
            product = jnp.zeros(total.shape, jnp.float32)
            for left, slab in zip(lefts, slabs):
                product = product + jnp.dot(
                    left,
                    every_solved[part, pl.ds(pl.multiple_of(slab * width, width), width), :],
                    preferred_element_type=jnp.float32,
                )
            out[0, :, columns] = total - product


def fused(factor, gradient):
    cycles, _, block, width = factor.shape
    columns = gradient.shape[3]
    heads = STEPS // ROWS
    chunk = columns // SPLIT
    items = heads + (cycles - heads) // GROUP
    panel = factor.reshape(cycles, block, width).astype(jnp.bfloat16)
    grad = gradient.reshape(cycles, block, columns)
    dma = pltpu.SemaphoreType.DMA
    any_spec = pl.BlockSpec(memory_space=pl.ANY)
    vmem_spec = pl.BlockSpec(memory_space=pltpu.VMEM)
    gathered, every_solved, own_solved = pl.pallas_call(
        solve_kernel,
        out_shape=(
            jax.ShapeDtypeStruct((COLS - 1, cycles - heads, block, width), jnp.bfloat16),
            jax.ShapeDtypeStruct((SPLIT, STEPS * block, chunk), jnp.bfloat16),
            jax.ShapeDtypeStruct((heads, block, columns), jnp.float32),
        ),
        in_specs=[any_spec, vmem_spec],
        out_specs=(any_spec, any_spec, vmem_spec),
        scratch_shapes=[
            pltpu.VMEM((COLS, heads, block, width), jnp.bfloat16),
            pltpu.VMEM((SPLIT, STEPS * block, chunk), jnp.bfloat16),
            pltpu.VMEM((heads, 2, HALF, HALF), jnp.float32),
        ]
        + [dma((items,))] * 6
        + [dma((STEPS * SPLIT,))] * 3
        + [dma((heads + 1,))],
        compiler_params=pltpu.CompilerParams(
            collective_id=0, has_side_effects=True, vmem_limit_bytes=56 * 1024 * 1024
        ),
    )(panel, grad[:heads])
    out = pl.pallas_call(
        functools.partial(trailing_kernel, heads),
        grid=(cycles,),
        out_shape=jax.ShapeDtypeStruct((cycles, block, columns), jnp.float32),
        in_specs=[
            pl.BlockSpec((1, block, width), lambda i: (jnp.maximum(i, heads), 0, 0)),
            pl.BlockSpec((COLS - 1, 1, block, width), lambda i: (0, jnp.maximum(i - heads, 0), 0, 0)),
            pl.BlockSpec((SPLIT, STEPS * block, chunk), lambda i: (0, 0, 0)),
            pl.BlockSpec((1, block, columns), lambda i: (jnp.minimum(i, heads - 1), 0, 0)),
            pl.BlockSpec((1, block, columns), lambda i: (i, 0, 0)),
        ],
        out_specs=pl.BlockSpec((1, block, columns), lambda i: (i, 0, 0)),
        compiler_params=pltpu.CompilerParams(
            dimension_semantics=("arbitrary",), vmem_limit_bytes=56 * 1024 * 1024
        ),
    )(panel, gathered, every_solved, own_solved, grad)
    return out.reshape(gradient.shape)


def local(factor, gradient):
    cycles, _, block, width = factor.shape
    fits = (
        lax.axis_size("row") == ROWS
        and lax.axis_size("col") == COLS
        and width == 2 * block
        and block == 2 * HALF
        and COLS * width == STEPS * block
        and (cycles - STEPS // ROWS) % GROUP == 0
    )
    return fused(factor, gradient) if fits else general(factor, gradient)


def solution(mesh):
    return jax.shard_map(
        local,
        mesh=mesh,
        in_specs=(P("layer", "row", None, "col"), P("layer", "row", None, "col")),
        out_specs=P("layer", "row", None, "col"),
        check_vma=False,
    )
```

```python
import functools

import jax
import jax.numpy as jnp
from jax import lax
from jax.experimental import pallas as pl
from jax.experimental.pallas import tpu as pltpu
from jax.sharding import PartitionSpec as P

STEPS = 8
ROWS = 4
COLS = 4
SPLIT = 8
HALF = 128
GROUP = 2
MESH = pl.DeviceIdType.MESH

def broadcast(shard, axis, root):
    mine = lax.axis_index(axis) == root
    return lax.psum(jnp.where(mine, shard, jnp.zeros_like(shard)), axis)


def general(factor, gradient):
    row_count = lax.axis_size("row")
    my_row = lax.axis_index("row")
    cycles, _, block_size, width_local = factor.shape
    blocks_per = width_local // block_size
    lowered = factor.reshape(cycles * block_size, width_local).astype(jnp.bfloat16)
    current = gradient.reshape(cycles * block_size, gradient.shape[3]).astype(jnp.float32)
    row_blocks = jnp.arange(cycles * block_size, dtype=jnp.int32) // block_size * row_count + my_row

    def fetch_tile(position):
        own_part = lax.dynamic_slice_in_dim(
            lowered, position % blocks_per * block_size, block_size, 1
        )
        return broadcast(own_part, "col", position // blocks_per)

    def own_rows(array, position):
        return lax.dynamic_slice_in_dim(array, position // row_count * block_size, block_size, 0)

    def solve_at(position, column_tile, right_side):
        diagonal = own_rows(column_tile, position).astype(jnp.float32)
        is_owner = position % row_count == my_row
        diagonal = jnp.where(is_owner, diagonal, jnp.eye(block_size, dtype=jnp.float32))
        return lax.linalg.triangular_solve(diagonal, right_side, left_side=True, lower=True)

    def share(solved, position):
        return broadcast(solved.astype(jnp.bfloat16), "row", position % row_count)

    def apply_block(current, position, column_tile, solved, sent_block):
        stored = lax.dynamic_update_slice_in_dim(
            current, solved, position // row_count * block_size, 0
        )
        is_owner = position % row_count == my_row
        current = jnp.where(is_owner, stored, current)
        product = jnp.dot(column_tile, sent_block, preferred_element_type=jnp.float32)
        pending = (row_blocks > position)[:, None]
        return current - jnp.where(pending, product, 0.0)

    def advance(position, current):
        column_tile = fetch_tile(position)
        solved = solve_at(position, column_tile, own_rows(current, position))
        sent_block = share(solved, position)
        return apply_block(current, position, column_tile, solved, sent_block)

    current = lax.fori_loop(0, STEPS, advance, current)
    return current.reshape(gradient.shape)


def exact_dot(a, b):
    return jnp.dot(a, b, precision=lax.Precision.HIGHEST, preferred_element_type=jnp.float32)


def invert_lower(lower):
    size = lower.shape[0]
    row = lax.broadcasted_iota(jnp.int32, (size, size), 0)
    col = lax.broadcasted_iota(jnp.int32, (size, size), 1)
    diagonal = jnp.where(row == col, lower, 0.0)
    scale_col = 1.0 / jnp.sum(diagonal, axis=0, keepdims=True)
    scale_row = 1.0 / jnp.sum(diagonal, axis=1, keepdims=True)
    pair = (row == col + 1) & (row % 2 == 1)
    inverse = jnp.where(row == col, scale_row, 0.0) - jnp.where(
        pair, scale_row * lower * scale_col, 0.0
    )
    width = 2
    while width < size:
        below = (
            (row // (2 * width) == col // (2 * width))
            & ((row // width) % 2 == 1)
            & ((col // width) % 2 == 0)
        )
        step = exact_dot(jnp.where(below, lower, 0.0), inverse)
        inverse = inverse - exact_dot(inverse, step)
        width *= 2
    return inverse


def solve_kernel(
    panel, gradient, gathered, every_solved, own_solved,
    grad, top, solved, inverse,
    x_send, x_recv, s_send, s_recv, f_send, f_recv,
    up_send, down_send, z_recv, local_sem,
):
    col = lax.axis_index("col")
    row = lax.axis_index("row")
    block = top.shape[2]
    chunk = solved.shape[2]
    heads = top.shape[1]
    groups = gathered.shape[1] // GROUP
    partner = (col + 2) % COLS
    sibling = col + 1 - 2 * (col % 2)

    barrier = pltpu.get_barrier_semaphore()
    for other in (partner, sibling):
        pl.semaphore_signal(barrier, inc=1, device_id={"col": other}, device_id_type=MESH)

    @pl.when(row > 0)
    def _():
        pl.semaphore_signal(barrier, inc=1, device_id={"row": row - 1}, device_id_type=MESH)

    @pl.when(row < ROWS - 1)
    def _():
        pl.semaphore_signal(barrier, inc=1, device_id={"row": row + 1}, device_id_type=MESH)

    inner = (row > 0) & (row < ROWS - 1)

    @pl.when(inner)
    def _():
        pl.semaphore_wait(barrier, 4)

    @pl.when(jnp.logical_not(inner))
    def _():
        pl.semaphore_wait(barrier, 3)

    def place(slab, slot, item):
        if isinstance(item, int) and item < heads:
            return top.at[slab, item]
        return gathered.at[slot, pl.ds((item - heads) * GROUP, GROUP)]

    def source(item):
        if isinstance(item, int) and item < heads:
            return panel.at[item]
        return panel.at[pl.ds(heads + (item - heads) * GROUP, GROUP)]

    def to_partner(item):
        return pltpu.make_async_remote_copy(
            src_ref=source(item), dst_ref=place(col, 0, item),
            send_sem=x_send.at[item], recv_sem=x_recv.at[item],
            device_id={"col": partner}, device_id_type=MESH,
        )

    def to_sibling(item):
        return pltpu.make_async_remote_copy(
            src_ref=source(item), dst_ref=place(col, 1, item),
            send_sem=s_send.at[item], recv_sem=s_recv.at[item],
            device_id={"col": sibling}, device_id_type=MESH,
        )

    def forward(item):
        return pltpu.make_async_remote_copy(
            src_ref=place(partner, 0, item), dst_ref=place(partner, 2, item),
            send_sem=f_send.at[item], recv_sem=f_recv.at[item],
            device_id={"col": sibling}, device_id_type=MESH,
        )

    def pass_on(item):
        to_partner(item).wait_recv()
        forward(item).start()

    def keep_head(item):
        return pltpu.make_async_copy(panel.at[item], top.at[col, item], local_sem.at[item])

    load_grad = pltpu.make_async_copy(
        gradient.at[pl.ds(0, heads)], grad, local_sem.at[heads]
    )
    for item in range(heads):
        to_partner(item).start()
        to_sibling(item).start()
        keep_head(item).start()
    load_grad.start()

    def receive_head(item):
        keep_head(item).wait()
        pass_on(item)
        to_sibling(item).wait_recv()
        forward(item).wait_recv()

    def invert(index):
        slab = row // 2 + 2 * index
        for half in range(2):
            start = pl.multiple_of((row % 2) * block + half * HALF, HALF)
            diagonal = top[slab, index, half * HALF:(half + 1) * HALF, pl.ds(start, HALF)]
            inverse[index, half] = invert_lower(diagonal.astype(jnp.float32))

    receive_head(0)

    @pl.loop(heads, heads + groups)
    def _(item):
        to_partner(item).start()

    invert(0)
    load_grad.wait()
    receive_head(1)

    @pl.when(row > 0)
    def _():
        invert(1)

    @pl.loop(heads, heads + groups)
    def _(item):
        to_sibling(item).start()

    def send_row(position, part, step, sems):
        piece = solved.at[part, pl.ds(position * block, block)]
        return pltpu.make_async_remote_copy(
            src_ref=piece, dst_ref=piece,
            send_sem=sems.at[position * SPLIT + part],
            recv_sem=z_recv.at[position * SPLIT + part],
            device_id={"row": row + step}, device_id_type=MESH,
        )

    def solve(position, part):
        index = position // ROWS
        columns = pl.ds(pl.multiple_of(part * chunk, chunk), chunk)
        right = grad[index, :, columns].astype(jnp.float32)
        width = top.shape[3]
        done = 0
        while done < position * block:
            take = min(width, position * block - done)
            right = right - jnp.dot(
                top[done // width, index, :, 0:take],
                solved[part, done:done + take, :],
                preferred_element_type=jnp.float32,
            )
            done += take
        first = exact_dot(inverse[index, 0], right[:HALF])
        slab, start = position * block // width, position * block % width
        below = top[slab, index, HALF:, start:start + HALF].astype(jnp.float32)
        second = exact_dot(inverse[index, 1], right[HALF:] - exact_dot(below, first))
        own_solved[index, :HALF, columns] = first
        own_solved[index, HALF:, columns] = second
        base = position * block
        solved[part, base:base + HALF, :] = first.astype(jnp.bfloat16)
        solved[part, base + HALF:base + block, :] = second.astype(jnp.bfloat16)

    def for_sends(position, part, act):
        owner = position % ROWS

        @pl.when((row >= owner) & (row < ROWS - 1))
        def _():
            act(send_row(position, part, 1, up_send))

        @pl.when((row <= owner) & (row > 0))
        def _():
            act(send_row(position, part, -1, down_send))

    starts = [0]
    for position in range(1, STEPS):
        hops = abs(position % ROWS - (position - 1) % ROWS)
        starts.append(starts[-1] + 1 + hops)
    ticks = starts[-1] + SPLIT + ROWS

    @pl.loop(0, ticks)
    def _(tick):
        for position in range(STEPS):
            hops = jnp.abs(row - position % ROWS)
            part = tick - starts[position] - jnp.where(hops == 0, 0, 1 + hops)

            @pl.when((part >= 0) & (part < SPLIT))
            def _():
                @pl.when(row == position % ROWS)
                def _():
                    solve(position, part)

                @pl.when(row != position % ROWS)
                def _():
                    send_row(position, part, 0, up_send).wait_recv()

                for_sends(position, part, lambda copy: copy.start())

        @pl.when((tick == SPLIT - 1) & (row == 0))
        def _():
            invert(1)

        @pl.when((tick % 4 == 3) & (tick // 4 < groups))
        def _():
            pass_on(heads + tick // 4)

    passed = min(groups, ticks // 4)

    def write_solved(part):
        columns = slice(part * chunk, (part + 1) * chunk)
        return pltpu.make_async_copy(
            solved.at[part], every_solved.at[:, columns], local_sem.at[heads + 1 + part]
        )

    for part in range(SPLIT):
        write_solved(part).start()

    @pl.loop(heads + passed, heads + groups)
    def _(item):
        pass_on(item)

    for item in range(heads):
        to_partner(item).wait_send()
        to_sibling(item).wait_send()
        forward(item).wait_send()

    @pl.loop(heads, heads + groups)
    def _(item):
        to_partner(item).wait_send()
        to_sibling(item).wait()
        forward(item).wait()

    for position in range(STEPS):
        @pl.loop(0, SPLIT)
        def _(part):
            for_sends(position, part, lambda copy: copy.wait_send())

    for part in range(SPLIT):
        write_solved(part).wait()


def trailing_kernel(heads, panel, gathered, every_solved, own_solved, grad, out):
    col = lax.axis_index("col")
    cycle = pl.program_id(0)

    @pl.when(cycle < heads)
    def _():
        out[0] = own_solved[0]

    @pl.when(cycle >= heads)
    def _():
        chunk = 2 * HALF
        width = gathered.shape[3]
        sibling = col + 1 - 2 * (col % 2)
        slabs = (col, (col + 2) % COLS, sibling, (sibling + 2) % COLS)
        lefts = (panel[0], gathered[0, 0], gathered[1, 0], gathered[2, 0])
        for part in range(every_solved.shape[1] // chunk):
            columns = slice(part * chunk, (part + 1) * chunk)
            total = grad[0, :, columns].astype(jnp.float32)
            product = jnp.zeros(total.shape, jnp.float32)
            for left, slab in zip(lefts, slabs):
                product = product + jnp.dot(
                    left,
                    every_solved[pl.ds(pl.multiple_of(slab * width, width), width), columns],
                    preferred_element_type=jnp.float32,
                )
            out[0, :, columns] = total - product


def fused(factor, gradient):
    cycles, _, block, width = factor.shape
    columns = gradient.shape[3]
    heads = STEPS // ROWS
    chunk = columns // SPLIT
    items = heads + (cycles - heads) // GROUP
    panel = factor.reshape(cycles, block, width).astype(jnp.bfloat16)
    grad = gradient.reshape(cycles, block, columns)
    dma = pltpu.SemaphoreType.DMA
    any_spec = pl.BlockSpec(memory_space=pl.ANY)
    vmem_spec = pl.BlockSpec(memory_space=pltpu.VMEM)
    gathered, every_solved, own_solved = pl.pallas_call(
        solve_kernel,
        out_shape=(
            jax.ShapeDtypeStruct((COLS - 1, cycles - heads, block, width), jnp.bfloat16),
            jax.ShapeDtypeStruct((STEPS * block, columns), jnp.bfloat16),
            jax.ShapeDtypeStruct((heads, block, columns), jnp.float32),
        ),
        in_specs=[any_spec, any_spec],
        out_specs=(any_spec, any_spec, vmem_spec),
        scratch_shapes=[
            pltpu.VMEM((heads, block, columns), jnp.bfloat16),
            pltpu.VMEM((COLS, heads, block, width), jnp.bfloat16),
            pltpu.VMEM((SPLIT, STEPS * block, chunk), jnp.bfloat16),
            pltpu.VMEM((heads, 2, HALF, HALF), jnp.float32),
        ]
        + [dma((items,))] * 6
        + [dma((STEPS * SPLIT,))] * 3
        + [dma((heads + 1 + SPLIT,))],
        compiler_params=pltpu.CompilerParams(
            collective_id=0, has_side_effects=True, vmem_limit_bytes=56 * 1024 * 1024
        ),
    )(panel, grad)
    out = pl.pallas_call(
        functools.partial(trailing_kernel, heads),
        grid=(cycles,),
        out_shape=jax.ShapeDtypeStruct((cycles, block, columns), jnp.float32),
        in_specs=[
            pl.BlockSpec((1, block, width), lambda i: (jnp.maximum(i, heads), 0, 0)),
            pl.BlockSpec((COLS - 1, 1, block, width), lambda i: (0, jnp.maximum(i - heads, 0), 0, 0)),
            pl.BlockSpec((STEPS * block, columns), lambda i: (0, 0)),
            pl.BlockSpec((1, block, columns), lambda i: (jnp.minimum(i, heads - 1), 0, 0)),
            pl.BlockSpec((1, block, columns), lambda i: (i, 0, 0)),
        ],
        out_specs=pl.BlockSpec((1, block, columns), lambda i: (i, 0, 0)),
        compiler_params=pltpu.CompilerParams(
            dimension_semantics=("arbitrary",), vmem_limit_bytes=56 * 1024 * 1024
        ),
    )(panel, gathered, every_solved, own_solved, grad)
    return out.reshape(gradient.shape)


def local(factor, gradient):
    cycles, _, block, width = factor.shape
    fits = (
        lax.axis_size("row") == ROWS
        and lax.axis_size("col") == COLS
        and width == 2 * block
        and block == 2 * HALF
        and COLS * width == STEPS * block
        and (cycles - STEPS // ROWS) % GROUP == 0
    )
    return fused(factor, gradient) if fits else general(factor, gradient)


def solution(mesh):
    return jax.shard_map(
        local,
        mesh=mesh,
        in_specs=(P("layer", "row", None, "col"), P("layer", "row", None, "col")),
        out_specs=P("layer", "row", None, "col"),
        check_vma=False,
    )
```

```python
import functools

import jax
import jax.numpy as jnp
from jax import lax
from jax.experimental import pallas as pl
from jax.experimental.pallas import tpu as pltpu
from jax.sharding import PartitionSpec as P

STEPS = 8
ROWS = 4
COLS = 4
SPLIT = 8
HALF = 128
GROUP = 2
MESH = pl.DeviceIdType.MESH

def broadcast(shard, axis, root):
    mine = lax.axis_index(axis) == root
    return lax.psum(jnp.where(mine, shard, jnp.zeros_like(shard)), axis)


def general(factor, gradient):
    row_count = lax.axis_size("row")
    my_row = lax.axis_index("row")
    cycles, _, block_size, width_local = factor.shape
    blocks_per = width_local // block_size
    lowered = factor.reshape(cycles * block_size, width_local).astype(jnp.bfloat16)
    current = gradient.reshape(cycles * block_size, gradient.shape[3]).astype(jnp.float32)
    row_blocks = jnp.arange(cycles * block_size, dtype=jnp.int32) // block_size * row_count + my_row

    def fetch_tile(position):
        own_part = lax.dynamic_slice_in_dim(
            lowered, position % blocks_per * block_size, block_size, 1
        )
        return broadcast(own_part, "col", position // blocks_per)

    def own_rows(array, position):
        return lax.dynamic_slice_in_dim(array, position // row_count * block_size, block_size, 0)

    def solve_at(position, column_tile, right_side):
        diagonal = own_rows(column_tile, position).astype(jnp.float32)
        is_owner = position % row_count == my_row
        diagonal = jnp.where(is_owner, diagonal, jnp.eye(block_size, dtype=jnp.float32))
        return lax.linalg.triangular_solve(diagonal, right_side, left_side=True, lower=True)

    def share(solved, position):
        return broadcast(solved.astype(jnp.bfloat16), "row", position % row_count)

    def apply_block(current, position, column_tile, solved, sent_block):
        stored = lax.dynamic_update_slice_in_dim(
            current, solved, position // row_count * block_size, 0
        )
        is_owner = position % row_count == my_row
        current = jnp.where(is_owner, stored, current)
        product = jnp.dot(column_tile, sent_block, preferred_element_type=jnp.float32)
        pending = (row_blocks > position)[:, None]
        return current - jnp.where(pending, product, 0.0)

    def advance(position, current):
        column_tile = fetch_tile(position)
        solved = solve_at(position, column_tile, own_rows(current, position))
        sent_block = share(solved, position)
        return apply_block(current, position, column_tile, solved, sent_block)

    current = lax.fori_loop(0, STEPS, advance, current)
    return current.reshape(gradient.shape)


def exact_dot(a, b):
    return jnp.dot(a, b, precision=lax.Precision.HIGHEST, preferred_element_type=jnp.float32)


def invert_lower(lower):
    size = lower.shape[0]
    row = lax.broadcasted_iota(jnp.int32, (size, size), 0)
    col = lax.broadcasted_iota(jnp.int32, (size, size), 1)
    diagonal = jnp.where(row == col, lower, 0.0)
    scale_col = 1.0 / jnp.sum(diagonal, axis=0, keepdims=True)
    scale_row = 1.0 / jnp.sum(diagonal, axis=1, keepdims=True)
    pair = (row == col + 1) & (row % 2 == 1)
    inverse = jnp.where(row == col, scale_row, 0.0) - jnp.where(
        pair, scale_row * lower * scale_col, 0.0
    )
    width = 2
    while width < size:
        below = (
            (row // (2 * width) == col // (2 * width))
            & ((row // width) % 2 == 1)
            & ((col // width) % 2 == 0)
        )
        step = exact_dot(jnp.where(below, lower, 0.0), inverse)
        inverse = inverse - exact_dot(inverse, step)
        width *= 2
    return inverse


def solve_kernel(
    panel, gradient, gathered, every_solved, own_solved,
    grad, top, solved, inverse,
    x_send, x_recv, s_send, s_recv, f_send, f_recv,
    up_send, down_send, z_recv, local_sem,
):
    col = lax.axis_index("col")
    row = lax.axis_index("row")
    block = top.shape[2]
    chunk = solved.shape[2]
    heads = top.shape[1]
    groups = gathered.shape[1] // GROUP
    partner = (col + 2) % COLS
    sibling = col + 1 - 2 * (col % 2)

    barrier = pltpu.get_barrier_semaphore()
    for other in (partner, sibling):
        pl.semaphore_signal(barrier, inc=1, device_id={"col": other}, device_id_type=MESH)

    @pl.when(row > 0)
    def _():
        pl.semaphore_signal(barrier, inc=1, device_id={"row": row - 1}, device_id_type=MESH)

    @pl.when(row < ROWS - 1)
    def _():
        pl.semaphore_signal(barrier, inc=1, device_id={"row": row + 1}, device_id_type=MESH)

    inner = (row > 0) & (row < ROWS - 1)

    @pl.when(inner)
    def _():
        pl.semaphore_wait(barrier, 4)

    @pl.when(jnp.logical_not(inner))
    def _():
        pl.semaphore_wait(barrier, 3)

    def place(slab, slot, item):
        if isinstance(item, int) and item < heads:
            return top.at[slab, item]
        return gathered.at[slot, pl.ds((item - heads) * GROUP, GROUP)]

    def source(item):
        if isinstance(item, int) and item < heads:
            return panel.at[item]
        return panel.at[pl.ds(heads + (item - heads) * GROUP, GROUP)]

    def to_partner(item):
        return pltpu.make_async_remote_copy(
            src_ref=source(item), dst_ref=place(col, 0, item),
            send_sem=x_send.at[item], recv_sem=x_recv.at[item],
            device_id={"col": partner}, device_id_type=MESH,
        )

    def to_sibling(item):
        return pltpu.make_async_remote_copy(
            src_ref=source(item), dst_ref=place(col, 1, item),
            send_sem=s_send.at[item], recv_sem=s_recv.at[item],
            device_id={"col": sibling}, device_id_type=MESH,
        )

    def forward(item):
        return pltpu.make_async_remote_copy(
            src_ref=place(partner, 0, item), dst_ref=place(partner, 2, item),
            send_sem=f_send.at[item], recv_sem=f_recv.at[item],
            device_id={"col": sibling}, device_id_type=MESH,
        )

    def pass_on(item):
        to_partner(item).wait_recv()
        forward(item).start()

    def keep_head(item):
        return pltpu.make_async_copy(panel.at[item], top.at[col, item], local_sem.at[item])

    load_grad = pltpu.make_async_copy(
        gradient.at[pl.ds(0, heads)], grad, local_sem.at[heads]
    )
    for item in range(heads):
        to_partner(item).start()
        to_sibling(item).start()
        keep_head(item).start()
    load_grad.start()

    def receive_head(item):
        keep_head(item).wait()
        pass_on(item)
        to_sibling(item).wait_recv()
        forward(item).wait_recv()

    def invert(index):
        slab = row // 2 + 2 * index
        for half in range(2):
            start = pl.multiple_of((row % 2) * block + half * HALF, HALF)
            diagonal = top[slab, index, half * HALF:(half + 1) * HALF, pl.ds(start, HALF)]
            inverse[index, half] = invert_lower(diagonal.astype(jnp.float32))

    receive_head(0)

    @pl.loop(heads, heads + groups)
    def _(item):
        to_partner(item).start()

    invert(0)
    load_grad.wait()
    receive_head(1)

    @pl.when(row > 0)
    def _():
        invert(1)

    @pl.loop(heads, heads + groups)
    def _(item):
        to_sibling(item).start()

    def send_row(position, part, step, sems):
        piece = solved.at[part, pl.ds(position * block, block)]
        return pltpu.make_async_remote_copy(
            src_ref=piece, dst_ref=piece,
            send_sem=sems.at[position * SPLIT + part],
            recv_sem=z_recv.at[position * SPLIT + part],
            device_id={"row": row + step}, device_id_type=MESH,
        )

    def solve(position, part):
        index = position // ROWS
        columns = pl.ds(pl.multiple_of(part * chunk, chunk), chunk)
        right = grad[index, :, columns].astype(jnp.float32)
        width = top.shape[3]
        done = 0
        while done < position * block:
            take = min(width, position * block - done)
            right = right - jnp.dot(
                top[done // width, index, :, 0:take],
                solved[part, done:done + take, :],
                preferred_element_type=jnp.float32,
            )
            done += take
        first = exact_dot(inverse[index, 0], right[:HALF])
        slab, start = position * block // width, position * block % width
        below = top[slab, index, HALF:, start:start + HALF].astype(jnp.float32)
        second = exact_dot(inverse[index, 1], right[HALF:] - exact_dot(below, first))
        own_solved[index, :HALF, columns] = first
        own_solved[index, HALF:, columns] = second
        base = position * block
        solved[part, base:base + HALF, :] = first.astype(jnp.bfloat16)
        solved[part, base + HALF:base + block, :] = second.astype(jnp.bfloat16)

    def for_sends(position, part, act):
        owner = position % ROWS

        @pl.when((row >= owner) & (row < ROWS - 1))
        def _():
            act(send_row(position, part, 1, up_send))

        @pl.when((row <= owner) & (row > 0))
        def _():
            act(send_row(position, part, -1, down_send))

    starts = [0]
    for position in range(1, STEPS):
        hops = abs(position % ROWS - (position - 1) % ROWS)
        starts.append(starts[-1] + 1 + hops)
    ticks = starts[-1] + SPLIT + ROWS

    @pl.loop(0, ticks)
    def _(tick):
        for position in range(STEPS):
            hops = jnp.abs(row - position % ROWS)
            part = tick - starts[position] - jnp.where(hops == 0, 0, 1 + hops)

            @pl.when((part >= 0) & (part < SPLIT))
            def _():
                @pl.when(row == position % ROWS)
                def _():
                    solve(position, part)

                @pl.when(row != position % ROWS)
                def _():
                    send_row(position, part, 0, up_send).wait_recv()

                for_sends(position, part, lambda copy: copy.start())

        @pl.when((tick == SPLIT - 1) & (row == 0))
        def _():
            invert(1)

        @pl.when((tick % 4 == 3) & (tick // 4 < groups))
        def _():
            pass_on(heads + tick // 4)

    passed = min(groups, ticks // 4)

    def write_solved(part):
        columns = slice(part * chunk, (part + 1) * chunk)
        return pltpu.make_async_copy(
            solved.at[part], every_solved.at[:, columns], local_sem.at[heads + 1 + part]
        )

    for part in range(SPLIT):
        write_solved(part).start()

    @pl.loop(heads + passed, heads + groups)
    def _(item):
        pass_on(item)

    for item in range(heads):
        to_partner(item).wait_send()
        to_sibling(item).wait_send()
        forward(item).wait_send()

    @pl.loop(heads, heads + groups)
    def _(item):
        to_partner(item).wait_send()
        to_sibling(item).wait()
        forward(item).wait()

    for position in range(STEPS):
        @pl.loop(0, SPLIT)
        def _(part):
            for_sends(position, part, lambda copy: copy.wait_send())

    for part in range(SPLIT):
        write_solved(part).wait()


def trailing_kernel(heads, panel, gathered, every_solved, own_solved, grad, out):
    col = lax.axis_index("col")
    step = pl.program_id(0)

    @pl.when(step < heads // GROUP)
    def _():
        out[...] = own_solved[...]

    @pl.when(step >= heads // GROUP)
    def _():
        chunk = 2 * HALF
        width = gathered.shape[3]
        sibling = col + 1 - 2 * (col % 2)
        slabs = (col, (col + 2) % COLS, sibling, (sibling + 2) % COLS)
        height = GROUP * panel.shape[1]
        lefts = [panel[...].reshape(height, width)]
        lefts += [gathered[slot].reshape(height, width) for slot in range(COLS - 1)]
        for part in range(every_solved.shape[1] // chunk):
            columns = slice(part * chunk, (part + 1) * chunk)
            total = grad[:, :, columns].reshape(height, chunk).astype(jnp.float32)
            product = jnp.zeros(total.shape, jnp.float32)
            for left, slab in zip(lefts, slabs):
                product = product + jnp.dot(
                    left,
                    every_solved[pl.ds(pl.multiple_of(slab * width, width), width), columns],
                    preferred_element_type=jnp.float32,
                )
            out[:, :, columns] = (total - product).reshape(GROUP, height // GROUP, chunk)


def fused(factor, gradient):
    cycles, _, block, width = factor.shape
    columns = gradient.shape[3]
    heads = STEPS // ROWS
    chunk = columns // SPLIT
    items = heads + (cycles - heads) // GROUP
    panel = factor.reshape(cycles, block, width).astype(jnp.bfloat16)
    grad = gradient.reshape(cycles, block, columns)
    dma = pltpu.SemaphoreType.DMA
    any_spec = pl.BlockSpec(memory_space=pl.ANY)
    vmem_spec = pl.BlockSpec(memory_space=pltpu.VMEM)
    gathered, every_solved, own_solved = pl.pallas_call(
        solve_kernel,
        out_shape=(
            jax.ShapeDtypeStruct((COLS - 1, cycles - heads, block, width), jnp.bfloat16),
            jax.ShapeDtypeStruct((STEPS * block, columns), jnp.bfloat16),
            jax.ShapeDtypeStruct((heads, block, columns), jnp.float32),
        ),
        in_specs=[any_spec, any_spec],
        out_specs=(any_spec, any_spec, vmem_spec),
        scratch_shapes=[
            pltpu.VMEM((heads, block, columns), jnp.bfloat16),
            pltpu.VMEM((COLS, heads, block, width), jnp.bfloat16),
            pltpu.VMEM((SPLIT, STEPS * block, chunk), jnp.bfloat16),
            pltpu.VMEM((heads, 2, HALF, HALF), jnp.float32),
        ]
        + [dma((items,))] * 6
        + [dma((STEPS * SPLIT,))] * 3
        + [dma((heads + 1 + SPLIT,))],
        compiler_params=pltpu.CompilerParams(
            collective_id=0, has_side_effects=True, vmem_limit_bytes=56 * 1024 * 1024
        ),
    )(panel, grad)
    out = pl.pallas_call(
        functools.partial(trailing_kernel, heads),
        grid=(cycles // GROUP,),
        out_shape=jax.ShapeDtypeStruct((cycles, block, columns), jnp.float32),
        in_specs=[
            pl.BlockSpec((GROUP, block, width), lambda i: (jnp.maximum(i, heads // GROUP), 0, 0)),
            pl.BlockSpec(
                (COLS - 1, GROUP, block, width),
                lambda i: (0, jnp.maximum(i - heads // GROUP, 0), 0, 0),
            ),
            pl.BlockSpec((STEPS * block, columns), lambda i: (0, 0)),
            pl.BlockSpec(
                (GROUP, block, columns), lambda i: (jnp.minimum(i, heads // GROUP - 1), 0, 0)
            ),
            pl.BlockSpec((GROUP, block, columns), lambda i: (i, 0, 0)),
        ],
        out_specs=pl.BlockSpec((GROUP, block, columns), lambda i: (i, 0, 0)),
        compiler_params=pltpu.CompilerParams(
            dimension_semantics=("arbitrary",), vmem_limit_bytes=56 * 1024 * 1024
        ),
    )(panel, gathered, every_solved, own_solved, grad)
    return out.reshape(gradient.shape)


def local(factor, gradient):
    cycles, _, block, width = factor.shape
    fits = (
        lax.axis_size("row") == ROWS
        and lax.axis_size("col") == COLS
        and width == 2 * block
        and block == 2 * HALF
        and COLS * width == STEPS * block
        and cycles % GROUP == 0
        and STEPS // ROWS % GROUP == 0
    )
    return fused(factor, gradient) if fits else general(factor, gradient)


def solution(mesh):
    return jax.shard_map(
        local,
        mesh=mesh,
        in_specs=(P("layer", "row", None, "col"), P("layer", "row", None, "col")),
        out_specs=P("layer", "row", None, "col"),
        check_vma=False,
    )
```
